32 devices in a mesh: groups: 2 (over y), seq: 4 (over x, core), heads: 4 (over z).
Axes of the slice: x: 2, y: 2, z: 4, core: 2. Of those that a mesh axis runs over, the one named last changes fastest.
Arguments:
- final_state: bfloat16 [2, 32, 1, 64, 80, 128], P(None, ('groups', 'seq', 'heads')), parts along dimension 1, may hold values from -2 to 2
- channel_tail: bfloat16 [2, 32, 1, 3, 5120], P(None, ('groups', 'seq', 'heads')), parts along dimension 1, may hold values from -6 to 6
- matrix_tail: bfloat16 [32, 1, 2, 3, 256], P(('groups', 'seq', 'heads')), parts along dimension 0, may hold values from -6 to 6
- last_hidden: bfloat16 [32, 1, 5120], P(('groups', 'seq', 'heads')), parts along dimension 0, may hold values from -6 to 6
- decode_group: int32 [32, 1], P(('groups', 'seq')), parts along dimension 0, may hold values from 0 to 3; in each aligned block of 4 rows (0 to 3, 4 to 7, ...) at most 2 rows name the same one
- input_weight: bfloat16 [2, 5120, 2, 5120], P(None, 'seq', None, 'heads'), may hold values from -0.078125 to 0.078125
- step_weight: bfloat16 [2, 5120, 64], P(None, 'seq', 'heads'), may hold values from -0.078125 to 0.078125
- matrix_weight: bfloat16 [2, 5120, 256], P(None, 'seq'), may hold values from -0.078125 to 0.078125
- channel_conv: float32 [2, 4, 5120], P(None, None, 'heads'), may hold values from -3 to 3
- matrix_conv: float32 [2, 4, 256], replicated, may hold values from -3 to 3
- step_bias: float32 [2, 64], P(None, 'heads'), may hold values from -4 to -1
- decay_log: float32 [2, 64], P(None, 'heads'), may hold values from 0 to 2.8
- skip_gain: float32 [2, 64], P(None, 'heads'), may hold values from 0.5 to 2
- norm_gain: float32 [2, 5120], P(None, 'heads'), may hold values from 0.25 to 1.75
- output_weight: bfloat16 [2, 5120, 5120], P(None, 'heads', 'seq'), may hold values from -0.078125 to 0.078125
Outputs:
- decoded: bfloat16 [64, 5120], P(('groups', 'heads'), 'seq'), parts along dimension 0
- new_state: bfloat16 [2, 8, 8, 64, 80, 128], P(None, ('groups', 'seq'), None, 'heads'), parts along dimension 1
The draws below stay inside these ranges and needn't reach their ends.
There are 2 independent parts, one for each index of `groups`. The reference program is written for one: setup_inputs(seed, part) draws one part's arguments, and reference() takes and returns one part's arrays. A program takes and returns all parts, laid end to end along the dimension named above; an argument that names none is the same for every part. Nothing has to cross between parts.
Inputs may be any that keep to these rules, and one draw needn't show every extreme that they name: `decode_group`: in each aligned block of 4 rows (the requests of one prefill row) no group is named more than 2 times; some group is named exactly 2 times in some block.
All inputs are finite; a program needn't handle non-finite values.
Results may differ from the reference program's by a relative error of at most 0.0065.
Values may be sent and summed in bfloat16 or wider, within the bound.
A program may use at most 128 MiB of HBM per device.

```python
import math
import jax
import jax.numpy as jnp
import numpy as np
from jax import lax

D = 5120
HEADS = 64
HEAD_DIM = 80
STATE = 128
KERNEL = 4
LAYERS = 2
SLOTS = 1
SHARDS = 16
REQUESTS = 16
BLOCK = 4
PAIR = 2
ROWCAP = 8
ROWS_ALL = 32
N_SEQ = 4


def steps_of(stream_key, dims, split, least, high):
    level = 1.0
    for axis_at, parts in split:
        steps = jax.random.uniform(jax.random.fold_in(jax.random.fold_in(stream_key, 6), axis_at), (parts,), jnp.float32, least / len(split), high / len(split))
        level = level * jnp.repeat(jnp.exp(steps), dims[axis_at] // parts).reshape((-1,) + (1,) * (len(dims) - 1 - axis_at))
    return level


def routed_block(stream_key, own, number, rows, number_of, top, limit, slope):
    sequence = jax.random.permutation(stream_key, number_of)
    packed, common = shares(number_of, rows * top, limit, slope, True), shares(number_of, rows * top, limit, slope, False)
    places = jnp.arange(number_of)

    def named(sizes, offset_by):
        used = int((sizes > 0).sum())
        fixed = max(1, used // 4)
        moved = fixed + (places - fixed + offset_by * (used - fixed)) % max(1, number_of - fixed)
        return jnp.zeros((number_of,), jnp.int32).at[sequence[jnp.where(places < fixed, places, moved)]].set(jnp.asarray(sizes, jnp.int32))

    sizes = jnp.where(number % 4 == 0, named(packed, number // 4), named(common, number - number // 4 - 1))
    mixed = jax.random.permutation(jax.random.fold_in(own, 3), number_of)
    donor, receiver = mixed[0:number_of // 2 * 2:2], mixed[1:number_of // 2 * 2:2]
    room = jnp.minimum(sizes[donor] - 1, limit - sizes[receiver]) // 2
    room = jnp.where((donor == sequence[0]) | (receiver == sequence[0]) | (sizes[receiver] == 0), 0, jnp.maximum(room, 0))
    moved = jax.random.randint(jax.random.fold_in(own, 4), (number_of // 2,), 0, 1 << 20) % (room + 1)
    sizes = sizes.at[donor].add(-moved).at[receiver].add(moved)
    labels = jnp.searchsorted(jnp.cumsum(sizes), jnp.arange(rows * top), side="right").astype(jnp.int32)
    listing = labels.reshape(top, rows).T
    listing = listing[jax.random.permutation(jax.random.fold_in(own, 1), rows)]
    offset_by = jax.random.randint(jax.random.fold_in(own, 2), (rows, 1), 0, top)
    return jnp.take_along_axis(listing, (jnp.arange(top)[None, :] + offset_by) % top, axis=1)


def shares(amount, total, bound, skew, full):
    portions = [(1 << 20) // math.isqrt(standing ** skew) + 1 for standing in range(1, amount + 1)]
    largest = bound if full else min(bound, max(-(-total // amount), total * portions[0] // sum(portions)))
    least = 1 if total - largest >= amount - 1 else 0
    holding, rest = [largest] + [least] * (amount - 1), total - largest - least * (amount - 1)
    while rest > 0:
        movable = [i for i in range(1, amount) if holding[i] < largest] or [i for i in range(1, amount) if holding[i] < bound]
        mass, left = sum([portions[i] for i in movable]), rest
        for i in movable:
            extra = min(bound - holding[i], max(1, left * portions[i] // mass), rest)
            holding[i] = holding[i] + extra
            rest = rest - extra
    return np.array(holding)


def noise(stream_key, dims, spread, limit, split=(), kind=jnp.bfloat16):
    loudness = steps_of(stream_key, dims, split, -0.22, 0.18) if split else 1.0
    result = jax.random.normal(stream_key, dims, jnp.float32) * spread * loudness
    return jnp.minimum(jnp.maximum(result, -limit), limit).astype(kind)


def setup_inputs(seed: int = 0, part: int = 0) -> dict:
    keys = jax.random.split(jax.random.key(seed), 16)
    part_keys = jax.random.split(jax.random.fold_in(keys[15], part), 16)
    final_state = noise(part_keys[0], (LAYERS, SHARDS, SLOTS, HEADS, HEAD_DIM, STATE), 0.3, 2.0, ((1, 16),))
    channel_tail = noise(part_keys[1], (LAYERS, SHARDS, SLOTS, KERNEL - 1, HEADS * HEAD_DIM), 1.0, 6.0, ((1, 16),))
    matrix_tail = noise(part_keys[2], (SHARDS, SLOTS, LAYERS, KERNEL - 1, 2 * STATE), 1.0, 6.0, ((0, 16),))
    last_hidden = noise(part_keys[3], (SHARDS, SLOTS, D), 1.0, 6.0, ((0, 16),))
    decode_group_keys = jax.random.split(jax.random.fold_in(part_keys[4], 1), REQUESTS // BLOCK)
    decode_group_turns = jax.random.permutation(jax.random.fold_in(part_keys[4], 3), REQUESTS // BLOCK)
    decode_group = jax.vmap(lambda own, number: routed_block(jax.random.fold_in(part_keys[4], 2), own, number, BLOCK, N_SEQ, 1, PAIR, 2))(decode_group_keys, decode_group_turns).reshape((REQUESTS, 1))
    input_weight = noise(keys[5], (LAYERS, D, 2, HEADS * HEAD_DIM), D ** -0.5, 0.078125, ((1, 4), (3, 4)))
    step_weight = noise(keys[6], (LAYERS, D, HEADS), D ** -0.5, 0.078125, ((1, 4), (2, 4)))
    matrix_weight = noise(keys[7], (LAYERS, D, 2 * STATE), D ** -0.5, 0.078125, ((1, 4),))
    channel_conv = noise(keys[8], (LAYERS, KERNEL, HEADS * HEAD_DIM), KERNEL ** -0.5, 3.0, ((2, 4),), jnp.float32)
    matrix_conv = noise(keys[9], (LAYERS, KERNEL, 2 * STATE), KERNEL ** -0.5, 3.0, (), jnp.float32)
    step_bias = jnp.clip(-4.0 + 3.0 * jax.random.uniform(keys[10], (LAYERS, HEADS), jnp.float32) ** steps_of(keys[10], (LAYERS, HEADS), ((1, 4),), -0.2, 0.2), -4.0, -1.0)
    decay_log = jnp.clip(2.8 * jax.random.uniform(keys[11], (LAYERS, HEADS), jnp.float32) ** steps_of(keys[11], (LAYERS, HEADS), ((1, 4),), -0.2, 0.2), 0.0, 2.8)
    skip_gain = jnp.clip(0.5 + 1.5 * jax.random.uniform(keys[12], (LAYERS, HEADS), jnp.float32) ** steps_of(keys[12], (LAYERS, HEADS), ((1, 4),), -0.2, 0.2), 0.5, 2.0)
    norm_gain = jnp.clip(1.0 + 0.15 * jax.random.normal(keys[13], (LAYERS, HEADS * HEAD_DIM), jnp.float32), 0.25, 1.75)
    output_weight = noise(keys[14], (LAYERS, HEADS * HEAD_DIM, D), (HEADS * HEAD_DIM) ** -0.5, 0.078125, ((1, 4), (2, 4)))
    return {"final_state": final_state, "channel_tail": channel_tail, "matrix_tail": matrix_tail, "last_hidden": last_hidden, "decode_group": decode_group, "input_weight": input_weight, "step_weight": step_weight, "matrix_weight": matrix_weight, "channel_conv": channel_conv, "matrix_conv": matrix_conv, "step_bias": step_bias, "decay_log": decay_log, "skip_gain": skip_gain, "norm_gain": norm_gain, "output_weight": output_weight}


def convolve(tail_block, taps_weight, fresh):
    kernel_taps = taps_weight.shape[0]
    summed = taps_weight[kernel_taps - 1] * fresh
    for tap_index in range(kernel_taps - 1):
        summed = summed + taps_weight[tap_index] * tail_block[:, tap_index].astype(jnp.float32)
    return jax.nn.silu(summed)

def reference(final_state, channel_tail, matrix_tail, last_hidden, decode_group, input_weight, step_weight, matrix_weight, channel_conv, matrix_conv, step_bias, decay_log, skip_gain, norm_gain, output_weight):
    member_ids = jnp.arange(REQUESTS, dtype=jnp.int32)
    prefill_row = member_ids // BLOCK
    dest_group = decode_group[:, 0].astype(jnp.int32)
    earlier = (prefill_row[:, None] == prefill_row[None, :]) & (dest_group[:, None] == dest_group[None, :]) & (member_ids[None, :] < member_ids[:, None])
    group_rank = lax.optimization_barrier(jnp.sum(earlier.astype(jnp.int32), axis=1)).astype(jnp.int32)
    dest_row = (dest_group * ROWCAP + prefill_row * PAIR + group_rank).astype(jnp.int32)
    hidden = last_hidden.reshape(REQUESTS, D)
    states_all = final_state.reshape(LAYERS, REQUESTS, HEADS, HEAD_DIM, STATE)
    chan_tails = channel_tail.reshape(LAYERS, REQUESTS, KERNEL - 1, HEADS * HEAD_DIM)
    mat_tails = matrix_tail.reshape(REQUESTS, LAYERS, KERNEL - 1, 2 * STATE)
    channels = HEADS * HEAD_DIM
    updated = []
    for layer_index in range(LAYERS):
        projected = jnp.dot(hidden, input_weight[layer_index].reshape(D, 2 * channels), preferred_element_type=jnp.float32)
        gate_part = projected[:, :channels]
        fresh_x = projected[:, channels:]
        step_raw = jnp.dot(hidden, step_weight[layer_index], preferred_element_type=jnp.float32)
        matrix_raw = jnp.dot(hidden, matrix_weight[layer_index], preferred_element_type=jnp.float32)
        conv_x = convolve(chan_tails[layer_index], channel_conv[layer_index], fresh_x)
        conv_matrix = convolve(mat_tails[:, layer_index], matrix_conv[layer_index], matrix_raw)
        input_matrix = conv_matrix[:, :STATE]
        output_matrix = conv_matrix[:, STATE:]
        step_size = jax.nn.softplus(step_raw + step_bias[layer_index])
        decay_rate = jnp.exp(-jnp.exp(decay_log[layer_index]) * step_size)
        head_x = conv_x.reshape(REQUESTS, HEADS, HEAD_DIM)

        def per_head(pieces):
            state_head, decay_head, step_head, x_head = pieces
            fresh_state = decay_head[:, None, None] * state_head.astype(jnp.float32) + (step_head[:, None] * x_head)[:, :, None] * input_matrix[:, None, :]
            read_out = jnp.einsum('rpn,rn->rp', fresh_state, output_matrix, precision=lax.Precision.HIGHEST)
            return (fresh_state.astype(jnp.bfloat16), read_out)
        head_states, head_out = lax.map(per_head, (jnp.transpose(states_all[layer_index], (1, 0, 2, 3)), decay_rate.T, step_size.T, jnp.transpose(head_x, (1, 0, 2))))
        updated.append(jnp.transpose(head_states, (1, 0, 2, 3)))
        y_heads = jnp.transpose(head_out, (1, 0, 2)) + skip_gain[layer_index][None, :, None] * head_x
        gated = y_heads.reshape(REQUESTS, channels) * jax.nn.silu(gate_part)
        mean_sq = lax.optimization_barrier(jnp.mean(gated * gated, axis=1, keepdims=True))
        normed = (gated * lax.rsqrt(mean_sq + 1e-05) * norm_gain[layer_index]).astype(jnp.bfloat16)
        out_sum = jnp.dot(normed, output_weight[layer_index], preferred_element_type=jnp.float32)
        hidden = (hidden.astype(jnp.float32) + out_sum).astype(jnp.bfloat16)
    decoded = jnp.zeros((ROWS_ALL, D), jnp.bfloat16).at[dest_row].set(hidden)
    stacked = jnp.stack(updated)
    new_state = jnp.zeros((LAYERS, ROWS_ALL, HEADS, HEAD_DIM, STATE), jnp.bfloat16).at[:, dest_row].set(stacked)
    return (decoded, new_state.reshape(LAYERS, N_SEQ, ROWCAP, HEADS, HEAD_DIM, STATE))
```

```python
import functools

import jax
import jax.numpy as jnp
from jax import lax
from jax.experimental import pallas as pl
from jax.experimental.pallas import tpu as pltpu
from jax.sharding import PartitionSpec as P

epsilon = 1e-05
f32 = jnp.float32
bf16 = jnp.bfloat16
MESH = pl.DeviceIdType.MESH


def silu(v):
    return v / (1.0 + jnp.exp(-v))


def kernel(
    dims,
    select_ref,
    state_hbm,
    tails_ref,
    mtails_ref,
    hidden_ref,
    rows_ref,
    win_hbm,
    wstep_hbm,
    wmat_hbm,
    cconv_ref,
    mconv_ref,
    sbias_ref,
    dlog_ref,
    skip_ref,
    ngain_ref,
    wout_hbm,
    decoded_ref,
    newstate_hbm,
    win,
    wout,
    wstep,
    wmat,
    outbox,
    hid_in,
    tails_in,
    mtails_in,
    rows_in,
    tails_rows,
    mtails_rows,
    current,
    spread,
    zx,
    zx_send,
    zx_recv,
    sm_send,
    sm_recv,
    flip_a,
    flip_b,
    col_a,
    col_b,
    col_y,
    gated_all,
    gated_send,
    ss_all,
    normed_ref,
    part,
    part_recv,
    result_send,
    local_sem,
    state_ssem,
    state_rsem,
    tok_ssem,
    tok_rsem,
    row_ssem,
    row_rsem,
    tail_ssem,
    tail_rsem,
    mt_ssem,
    mt_rsem,
    zx_ssem,
    zx_rsem,
    sm_ssem,
    sm_rsem,
    g_ssem,
    g_rsem,
    ss_ssem,
    ss_rsem,
    part_ssem,
    part_rsem,
    res_ssem,
    res_rsem,
    out_ssem,
    out_rsem,
    *state,
):
    layers, heads_n, seq_n, members, head_dev, head_width, width, channels, pair, taps = dims
    requests = seq_n * members
    chunk_rows = requests // heads_n
    share_rows = decoded_ref.shape[0]
    model_width = width * seq_n
    s_me = lax.axis_index("seq")
    h_me = lax.axis_index("heads")
    me = s_me * heads_n + h_me
    devices = seq_n * heads_n
    channels_pad = flip_a.shape[1]

    loads = []

    def load(src, dst, index):
        copy = pltpu.make_async_copy(src, dst, local_sem.at[index])
        copy.start()
        return copy

    def peer(offset):
        other = lax.rem(me + offset, devices)
        return other // heads_n, lax.rem(other, heads_n)

    win_load = [load(win_hbm.at[l], win.at[l], l) for l in range(layers)]
    wout_load = [load(wout_hbm.at[l], wout.at[l], layers + l) for l in range(layers)]
    wstep_load = load(wstep_hbm, wstep, 2 * layers)
    wmat_load = load(wmat_hbm, wmat, 2 * layers + 1)
    own_load = [
        load(
            state_hbm.at[l, 0, 0, pl.ds(h_me * head_dev, head_dev)],
            state[l].at[h_me],
            2 * layers + 2 + l,
        )
        for l in range(layers)
    ]

    barrier = pltpu.get_barrier_semaphore()

    @pl.loop(1, devices)
    def _(offset):
        s_to, h_to = peer(offset)
        pl.semaphore_signal(
            barrier, inc=1, device_id={"seq": s_to, "heads": h_to}, device_id_type=MESH
        )

    pl.semaphore_wait(barrier, devices - 1)

    pending = []

    def remote(src, dst, ssem, rsem, where):
        copy = pltpu.make_async_remote_copy(
            src_ref=src,
            dst_ref=dst,
            send_sem=ssem,
            recv_sem=rsem,
            device_id=where,
            device_id_type=MESH,
        )
        copy.start()
        pending.append(copy)
        return copy

    def token_copy(offset):
        s_to, h_to = peer(offset)
        return pltpu.make_async_remote_copy(
            src_ref=hidden_ref.at[s_to],
            dst_ref=hid_in.at[me],
            send_sem=tok_ssem.at[offset],
            recv_sem=tok_rsem.at[offset],
            device_id={"seq": s_to, "heads": h_to},
            device_id_type=MESH,
        )

    @pl.loop(1, devices)
    def _(offset):
        token_copy(offset).start()

    row_copies = [
        remote(
            rows_ref,
            rows_in.at[s_me],
            row_ssem.at[d],
            row_rsem.at[d],
            {"seq": lax.rem(s_me + d, seq_n)},
        )
        for d in range(1, seq_n)
    ]
    tail_copies = []
    for d in range(1, heads_n):
        h_to = lax.rem(h_me + d, heads_n)
        tail_copies.append(
            remote(
                tails_ref.at[h_to],
                tails_in.at[h_me],
                tail_ssem.at[d],
                tail_rsem.at[d],
                {"heads": h_to},
            )
        )
        tail_copies.append(
            remote(
                mtails_ref, mtails_in.at[h_me], mt_ssem.at[d], mt_rsem.at[d], {"heads": h_to}
            )
        )

    def send_state(l):
        copies = []
        for d in range(1, heads_n):
            h_to = lax.rem(h_me + d, heads_n)
            copies.append(
                remote(
                    state_hbm.at[l, 0, 0, pl.ds(h_to * head_dev, head_dev)],
                    state[l].at[h_me],
                    state_ssem.at[l, d],
                    state_rsem.at[l, d],
                    {"heads": h_to},
                )
            )
        return copies

    state_copies = {0: send_state(0)}

    hid_in[me] = hidden_ref[s_me]
    rows_in[s_me] = rows_ref[...]
    tails_in[h_me] = tails_ref[h_me]
    mtails_in[h_me] = mtails_ref[...]

    @pl.loop(1, devices)
    def _(offset):
        token_copy(offset).wait_recv()

    for r in range(requests):
        current[r // chunk_rows, r % chunk_rows : r % chunk_rows + 1, :] = hid_in[r]

    even = lax.broadcasted_iota(jnp.int32, (128, 256), 1) - 2 * lax.broadcasted_iota(
        jnp.int32, (128, 256), 0
    )
    pick = [(even == 0).astype(bf16), (even == 1).astype(bf16)]
    expand = lax.broadcasted_iota(jnp.int32, (head_dev, channels), 1) - head_width * (
        lax.broadcasted_iota(jnp.int32, (head_dev, channels), 0)
    )
    expand = ((expand >= 0) & (expand < head_width)).astype(f32)

    def per_channel(values):
        return jnp.dot(
            values, expand, precision=lax.Precision.HIGHEST, preferred_element_type=f32
        )

    block = 256 if channels % 256 == 0 else channels
    block_out = 256 if width % 256 == 0 else width
    group_heads = 4 if head_dev % 4 == 0 else head_dev
    group_rows = group_heads * head_width

    for l in range(layers):
        hidden = jnp.concatenate([current[c] for c in range(heads_n)], axis=0).astype(bf16)
        for k in range(width // 128):
            part_h = hidden[:, k * 128 : (k + 1) * 128]
            for half in range(2):
                spread[half * requests : (half + 1) * requests, k * 256 : (k + 1) * 256] = jnp.dot(
                    part_h, pick[half], preferred_element_type=f32
                ).astype(bf16)
        win_load[l].wait()
        weight = win.at[l].reshape(2 * width, channels)
        if block == channels:
            zx[...] = jnp.dot(spread[...], weight[...], preferred_element_type=f32)
        else:

            @pl.loop(0, channels // block)
            def _(n):
                cols = pl.ds(pl.multiple_of(n * block, block), block)
                zx[:, cols] = jnp.dot(spread[...], weight[:, cols], preferred_element_type=f32)

        if l == 0:
            wstep_load.wait()
            wmat_load.wait()
        step_part = jnp.dot(hidden, wstep[l], preferred_element_type=f32)
        mat_part = jnp.dot(hidden, wmat[l], preferred_element_type=f32)
        for q in range(seq_n):
            rows = slice(q * members, (q + 1) * members)
            zx_send[l, q, 0] = zx[q * members : (q + 1) * members, :]
            zx_send[l, q, 1] = zx[requests + q * members : requests + (q + 1) * members, :]
            sm_send[l, q, :, 0:256] = mat_part[rows]
            sm_send[l, q, :, 256 : 256 + head_dev] = step_part[rows]
        copies = []
        for d in range(1, seq_n):
            s_to = lax.rem(s_me + d, seq_n)
            copies.append(
                remote(
                    zx_send.at[l, s_to],
                    zx_recv.at[l, d],
                    zx_ssem.at[l, d],
                    zx_rsem.at[l, d],
                    {"seq": s_to},
                )
            )
            copies.append(
                remote(
                    sm_send.at[l, s_to],
                    sm_recv.at[l, d],
                    sm_ssem.at[l, d],
                    sm_rsem.at[l, d],
                    {"seq": s_to},
                )
            )
        if l == 0:
            for copy in tail_copies + row_copies:
                copy.wait_recv()
            for m in range(members):
                for i in range(layers * (taps - 1)):
                    tails_rows[i, m : m + 1, :] = tails_in[m, i : i + 1, :]
                    mtails_rows[i, m : m + 1, :] = mtails_in[m, i : i + 1, :]
        for copy in copies:
            copy.wait_recv()
        zx_sum = zx_send[l, s_me]
        sm_sum = sm_send[l, s_me]
        for d in range(1, seq_n):
            zx_sum = zx_sum + zx_recv[l, d]
            sm_sum = sm_sum + sm_recv[l, d]
        gate = zx_sum[0]
        conv_x = cconv_ref[l, taps - 1 : taps, :] * zx_sum[1]
        conv_m = mconv_ref[l, taps - 1 : taps, :] * sm_sum[:, 0:256]
        for j in range(taps - 1):
            conv_x = conv_x + cconv_ref[l, j : j + 1, :] * tails_rows[l * (taps - 1) + j]
            conv_m = conv_m + mconv_ref[l, j : j + 1, :] * mtails_rows[l * (taps - 1) + j]
        conv_x = silu(conv_x)
        conv_m = silu(conv_m)
        half_m = conv_m.shape[1] // 2
        step_in = sm_sum[:, 256 : 256 + head_dev] + sbias_ref[l : l + 1, :]
        step = jnp.maximum(step_in, 0.0) + jnp.log1p(jnp.exp(-jnp.abs(step_in)))
        decay = jnp.exp(-jnp.exp(dlog_ref[l : l + 1, :]) * step)
        flip_a[0:members, 0:channels] = per_channel(decay)
        flip_b[0:members, 0:channels] = per_channel(step) * conv_x
        skip = per_channel(jnp.broadcast_to(skip_ref[l : l + 1, :], (8, head_dev)))[0:1]
        for k in range(channels_pad // 128):
            cols = slice(k * 128, (k + 1) * 128)
            col_a[cols, :] = flip_a[:, cols].T
            col_b[cols, :] = flip_b[:, cols].T

        own_load[l].wait()
        for copy in state_copies[l]:
            copy.wait_recv()
        if l + 1 < layers:
            state_copies[l + 1] = send_state(l + 1)

        lane = lax.broadcasted_iota(jnp.int32, (group_rows, 128), 1)

        @pl.loop(0, head_dev // group_heads)
        def _(i):
            rows = pl.ds(pl.multiple_of(i * group_rows, 8), group_rows)
            heads = pl.ds(i * group_heads, group_heads)
            total = jnp.zeros((group_rows, 128), f32)
            for m in range(members):
                old = state[l][m, heads].reshape(group_rows, half_m).astype(f32)
                fresh = (
                    col_a[rows, m : m + 1] * old
                    + col_b[rows, m : m + 1] * conv_m[m : m + 1, 0:half_m]
                )
                read = jnp.sum(fresh * conv_m[m : m + 1, half_m:], axis=1, keepdims=True)
                total = jnp.where(lane == m, read, total)
                state[l][m, heads] = fresh.astype(bf16).reshape(group_heads, head_width, half_m)
            col_y[rows, :] = total

        for k in range(channels_pad // 128):
            cols = slice(k * 128, (k + 1) * 128)
            flip_a[:, cols] = col_y[cols, :].T
        gated = (flip_a[0:members, 0:channels] + skip * conv_x) * silu(gate)
        gated_send[l] = gated
        gated_all[l, s_me] = gated
        square = jnp.broadcast_to(jnp.sum(gated * gated, axis=1, keepdims=True), (members, 128))
        ss_all[l, me] = square
        g_copies = []
        for d in range(1, seq_n):
            g_copies.append(
                remote(
                    gated_send.at[l],
                    gated_all.at[l, s_me],
                    g_ssem.at[l, d],
                    g_rsem.at[l, d],
                    {"seq": lax.rem(s_me + d, seq_n)},
                )
            )

        def square_copy(offset):
            s_to, h_to = peer(offset)
            return pltpu.make_async_remote_copy(
                src_ref=ss_all.at[l, me],
                dst_ref=ss_all.at[l, me],
                send_sem=ss_ssem.at[l, offset],
                recv_sem=ss_rsem.at[l, offset],
                device_id={"seq": s_to, "heads": h_to},
                device_id_type=MESH,
            )

        @pl.loop(1, devices)
        def _(offset):
            square_copy(offset).start()

        def send_rows():
            @pl.loop(0, seq_n * pair)
            def _(slot):
                source = select_ref[0, slot]
                keep = select_ref[1, slot].astype(f32).astype(bf16)
                q_to = slot // pair
                k_to = lax.rem(slot, pair)

                @pl.loop(0, head_dev // group_heads)
                def _(i):
                    heads = pl.ds(i * group_heads, group_heads)
                    outbox[l, q_to, k_to, heads] = state[l][source, heads] * keep

            for d in range(1, seq_n):
                s_to = lax.rem(s_me + d, seq_n)
                remote(
                    outbox.at[l, s_to],
                    newstate_hbm.at[l, 0, pl.ds(s_me * pair, pair)],
                    out_ssem.at[l, d],
                    out_rsem.at[l, d],
                    {"seq": s_to},
                )
            own = pltpu.make_async_copy(
                outbox.at[l, s_me],
                newstate_hbm.at[l, 0, pl.ds(s_me * pair, pair)],
                local_sem.at[3 * layers + 2 + l],
            )
            own.start()
            loads.append(own)

        send_rows()

        for copy in g_copies:
            copy.wait_recv()

        @pl.loop(1, devices)
        def _(offset):
            square_copy(offset).wait()

        for q in range(seq_n):
            total_sq = ss_all[l, q * heads_n]
            for h in range(1, heads_n):
                total_sq = total_sq + ss_all[l, q * heads_n + h]
            scale = lax.rsqrt(total_sq[:, 0:1] / model_width + epsilon)
            normed_ref[q * members : (q + 1) * members, :] = (
                gated_all[l, q] * scale * ngain_ref[l : l + 1, :]
            )
        wout_load[l].wait()
        normed = normed_ref[...].astype(bf16)
        if block_out == width:
            zout = jnp.dot(normed, wout[l], preferred_element_type=f32)
            for c in range(heads_n):
                part[l, c] = zout[c * chunk_rows : (c + 1) * chunk_rows]
        else:

            @pl.loop(0, width // block_out)
            def _(n):
                cols = pl.ds(pl.multiple_of(n * block_out, block_out), block_out)
                zout = jnp.dot(normed, wout[l, :, cols], preferred_element_type=f32)
                for c in range(heads_n):
                    part[l, c, :, cols] = zout[c * chunk_rows : (c + 1) * chunk_rows]

        copies = []
        for d in range(1, heads_n):
            h_to = lax.rem(h_me + d, heads_n)
            copies.append(
                remote(
                    part.at[l, h_to],
                    part_recv.at[l, d],
                    part_ssem.at[l, d],
                    part_rsem.at[l, d],
                    {"heads": h_to},
                )
            )
        for copy in copies:
            copy.wait_recv()
        summed = part[l, h_me]
        for d in range(1, heads_n):
            summed = summed + part_recv[l, d]
        base = current if l == 0 else result_send.at[l - 1]
        result_send[l, h_me] = (base[h_me] + summed).astype(bf16).astype(f32)
        copies = []
        for d in range(1, heads_n):
            h_to = lax.rem(h_me + d, heads_n)
            copies.append(
                remote(
                    result_send.at[l, h_me],
                    result_send.at[l, h_me],
                    res_ssem.at[l, d],
                    res_rsem.at[l, d],
                    {"heads": h_to},
                )
            )
        for copy in copies:
            copy.wait_recv()
        current_next = result_send.at[l]
        if l + 1 < layers:
            for c in range(heads_n):
                current[c] = current_next[c]
            if l == 0:
                pass

    final = jnp.concatenate([result_send[layers - 1, c] for c in range(heads_n)], axis=0)
    targets = jnp.concatenate([rows_in[q] for q in range(seq_n)], axis=0)
    wanted = (h_me * share_rows).astype(f32) + lax.broadcasted_iota(
        jnp.int32, (requests, 128), 1
    ).astype(f32)
    hot = (targets == wanted).astype(f32).astype(bf16)
    chosen = lax.dot_general(
        hot, final.astype(bf16), (((0,), (0,)), ((), ())), preferred_element_type=f32
    )
    decoded_ref[...] = chosen[0:share_rows].astype(bf16)

    @pl.loop(1, devices)
    def _(offset):
        token_copy(offset).wait_send()

    for copy in loads:
        copy.wait()
    for copy in pending:
        copy.wait_send()
    for l in range(layers):
        for d in range(1, seq_n):
            pltpu.make_async_remote_copy(
                src_ref=outbox.at[l, s_me],
                dst_ref=newstate_hbm.at[
                    l, 0, pl.ds(lax.rem(s_me + seq_n - d, seq_n) * pair, pair)
                ],
                send_sem=out_ssem.at[l, d],
                recv_sem=out_rsem.at[l, d],
                device_id={"seq": lax.rem(s_me + d, seq_n)},
                device_id_type=MESH,
            ).wait_recv()


def on_device(
    final_state,
    channel_tail,
    matrix_tail,
    last_hidden,
    decode_group,
    input_weight,
    step_weight,
    matrix_weight,
    channel_conv,
    matrix_conv,
    step_bias,
    decay_log,
    skip_gain,
    norm_gain,
    output_weight,
):
    heads_n = lax.axis_size("heads")
    seq_n = lax.axis_size("seq")
    layers, _, slots, heads_all, head_width, state_width = final_state.shape
    head_dev = heads_all // heads_n
    model_width = last_hidden.shape[2]
    width = model_width // seq_n
    taps = channel_conv.shape[1]
    members = heads_n * slots
    pair = 2 * members // seq_n
    capacity = seq_n * pair
    requests = seq_n * members
    share_rows = capacity * seq_n // heads_n
    chunk_rows = requests // heads_n
    channels = head_dev * head_width
    channels_pad = -(-channels // 128) * 128
    tail_rows = layers * (taps - 1)
    devices = seq_n * heads_n

    dest = decode_group[:, 0]
    member_ids = jnp.arange(members, dtype=jnp.int32)
    earlier = (dest[:, None] == dest[None, :]) & (member_ids[None, :] < member_ids[:, None])
    rank = jnp.sum(earlier.astype(jnp.int32), axis=1)
    target = dest * pair + rank
    matches = target[None, :] == jnp.arange(capacity, dtype=jnp.int32)[:, None]
    source = jnp.sum(jnp.where(matches, member_ids[None, :], 0), axis=1)
    filled = jnp.sum(matches.astype(jnp.int32), axis=1)
    select = jnp.stack([source, filled])
    row = dest * capacity + lax.axis_index("seq") * pair + rank
    rows = jnp.broadcast_to(row.astype(f32)[:, None], (members, 128))

    tails = jnp.transpose(
        channel_tail.reshape(tail_rows, heads_n, channels), (1, 0, 2)
    ).astype(f32)
    mtails = matrix_tail.reshape(tail_rows, 2 * state_width).astype(f32)
    hidden = last_hidden.reshape(seq_n, 1, width).astype(f32)

    dims = (
        layers, heads_n, seq_n, members, head_dev, head_width, width, channels, pair, taps
    )
    vmem = pl.BlockSpec(memory_space=pltpu.VMEM)
    smem = pl.BlockSpec(memory_space=pltpu.SMEM)
    anyw = pl.BlockSpec(memory_space=pl.ANY)
    V = pltpu.VMEM
    dma = pltpu.SemaphoreType.DMA
    scratch = [
        V((layers, width, 2, channels), bf16),
        V((layers, channels, width), bf16),
        V((layers, width, head_dev), bf16),
        V((layers, width, 2 * state_width), bf16),
        V((layers, seq_n, pair, head_dev, head_width, state_width), bf16),
        V((requests, 1, width), f32),
        V((heads_n, tail_rows, channels), f32),
        V((heads_n, tail_rows, 2 * state_width), f32),
        V((seq_n, members, 128), f32),
        V((tail_rows, members, channels), f32),
        V((tail_rows, members, 2 * state_width), f32),
        V((heads_n, chunk_rows, width), f32),
        V((2 * requests, 2 * width), bf16),
        V((2 * requests, channels), f32),
        V((layers, seq_n, 2, members, channels), f32),
        V((layers, seq_n, 2, members, channels), f32),
        V((layers, seq_n, members, 384), f32),
        V((layers, seq_n, members, 384), f32),
        V((128, channels_pad), f32),
        V((128, channels_pad), f32),
        V((channels_pad, 128), f32),
        V((channels_pad, 128), f32),
        V((channels_pad, 128), f32),
        V((layers, seq_n, members, channels), f32),
        V((layers, members, channels), f32),
        V((layers, devices, members, 128), f32),
        V((requests, channels), f32),
        V((layers, heads_n, chunk_rows, width), f32),
        V((layers, heads_n, chunk_rows, width), f32),
        V((layers, heads_n, chunk_rows, width), f32),
        dma((4 * layers + 2,)),
        dma((layers, heads_n)),
        dma((layers, heads_n)),
        dma((devices,)),
        dma((devices,)),
        dma((seq_n,)),
        dma((seq_n,)),
        dma((heads_n,)),
        dma((heads_n,)),
        dma((heads_n,)),
        dma((heads_n,)),
        dma((layers, seq_n)),
        dma((layers, seq_n)),
        dma((layers, seq_n)),
        dma((layers, seq_n)),
        dma((layers, seq_n)),
        dma((layers, seq_n)),
        dma((layers, devices)),
        dma((layers, devices)),
        dma((layers, heads_n)),
        dma((layers, heads_n)),
        dma((layers, heads_n)),
        dma((layers, heads_n)),
        dma((layers, seq_n)),
        dma((layers, seq_n)),
    ] + [V((members, head_dev, head_width, state_width), bf16) for _ in range(layers)]
    decoded, new_state = pl.pallas_call(
        functools.partial(kernel, dims),
        out_shape=(
            jax.ShapeDtypeStruct((share_rows, width), bf16),
            jax.ShapeDtypeStruct(
                (layers, 1, capacity, head_dev, head_width, state_width), bf16
            ),
        ),
        in_specs=[
            smem, anyw, vmem, vmem, vmem, vmem, anyw, anyw, anyw,
            vmem, vmem, vmem, vmem, vmem, vmem, anyw,
        ],
        out_specs=(vmem, anyw),
        scratch_shapes=scratch,
        compiler_params=pltpu.CompilerParams(
            collective_id=0, has_side_effects=True, vmem_limit_bytes=58 * 1024 * 1024
        ),
        cost_estimate=pl.CostEstimate(
            flops=4 * requests * width * channels * 3 * layers,
            bytes_accessed=30_000_000,
            transcendentals=0,
        ),
        name="handover",
    )(
        select,
        final_state,
        tails,
        mtails,
        hidden,
        rows,
        input_weight,
        step_weight,
        matrix_weight,
        channel_conv,
        matrix_conv,
        step_bias,
        decay_log,
        skip_gain,
        norm_gain,
        output_weight,
    )
    return decoded, new_state


def solution(mesh):
    return jax.shard_map(
        on_device,
        mesh=mesh,
        in_specs=(
            P(None, ("groups", "seq", "heads"), None, None, None, None),
            P(None, ("groups", "seq", "heads"), None, None, None),
            P(("groups", "seq", "heads"), None, None, None, None),
            P(("groups", "seq", "heads"), None, None),
            P(("groups", "seq"), None),
            P(None, "seq", None, "heads"),
            P(None, "seq", "heads"),
            P(None, "seq", None),
            P(None, None, "heads"),
            P(),
            P(None, "heads"),
            P(None, "heads"),
            P(None, "heads"),
            P(None, "heads"),
            P(None, "heads", "seq"),
        ),
        out_specs=(
            P(("groups", "heads"), "seq"),
            P(None, ("groups", "seq"), None, "heads", None, None),
        ),
        check_vma=False,
    )
```

```python
import functools

import jax
import jax.numpy as jnp
from jax import lax
from jax.experimental import pallas as pl
from jax.experimental.pallas import tpu as pltpu
from jax.sharding import PartitionSpec as P

epsilon = 1e-05
f32 = jnp.float32
bf16 = jnp.bfloat16
MESH = pl.DeviceIdType.MESH


def silu(v):
    return v / (1.0 + jnp.exp(-v))


def kernel(
    dims,
    group_ref,
    state_hbm,
    tails_arg,
    mtails_arg,
    hidden_arg,
    win_hbm,
    wstep_hbm,
    wmat_hbm,
    cconv_ref,
    mconv_ref,
    sbias_ref,
    dlog_ref,
    skip_ref,
    ngain_ref,
    wout_hbm,
    decoded_ref,
    raw_hbm,
    vec_hbm,
    win,
    wout,
    wstep,
    wmat,
    outbox,
    hid_in,
    tails_in,
    mtails_in,
    rows_in,
    tails_rows,
    mtails_rows,
    current,
    spread,
    zx,
    zx_send,
    zx_recv,
    sm_send,
    sm_recv,
    flip_a,
    col_y,
    tails_ref,
    mtails_ref,
    hidden_ref,
    rows_ref,
    vec_rows,
    vec_send,
    gated_all,
    gated_send,
    ss_all,
    normed_ref,
    part,
    part_recv,
    result_send,
    local_sem,
    state_ssem,
    state_rsem,
    tok_ssem,
    tok_rsem,
    row_ssem,
    row_rsem,
    tail_ssem,
    tail_rsem,
    mt_ssem,
    mt_rsem,
    zx_ssem,
    zx_rsem,
    sm_ssem,
    sm_rsem,
    g_ssem,
    g_rsem,
    ss_ssem,
    ss_rsem,
    part_ssem,
    part_rsem,
    res_ssem,
    res_rsem,
    out_ssem,
    out_rsem,
    vec_ssem,
    vec_rsem,
    *state_flat,
):
    layers, heads_n, seq_n, members, head_dev, head_width, width, channels, pair, taps = dims
    requests = seq_n * members
    chunk_rows = requests // heads_n
    share_rows = decoded_ref.shape[0]
    model_width = width * seq_n
    s_me = lax.axis_index("seq")
    h_me = lax.axis_index("heads")
    me = s_me * heads_n + h_me
    devices = seq_n * heads_n
    channels_pad = flip_a.shape[1]
    group_heads = 4 if head_dev % 4 == 0 else head_dev
    group_rows = group_heads * head_width
    chunks = head_dev // group_heads
    steps = [(l, c) for l in range(layers) for c in range(chunks)]
    state = [[state_flat[l * chunks + c] for c in range(chunks)] for l in range(layers)]
    capacity = seq_n * pair

    loads = []

    def load(src, dst, index):
        copy = pltpu.make_async_copy(src, dst, local_sem.at[index])
        copy.start()
        return copy

    def peer(offset):
        other = lax.rem(me + offset, devices)
        return other // heads_n, lax.rem(other, heads_n)

    win_load = [load(win_hbm.at[l], win.at[l], l) for l in range(layers)]
    wout_load = [load(wout_hbm.at[l], wout.at[l], layers + l) for l in range(layers)]
    wstep_load = load(wstep_hbm, wstep, 2 * layers)
    wmat_load = load(wmat_hbm, wmat, 2 * layers + 1)
    own_load = [
        load(
            state_hbm.at[l, 0, 0, pl.ds(h_me * head_dev + c * group_heads, group_heads)],
            state[l][c].at[h_me],
            2 * layers + 2 + l * chunks + c,
        )
        for l, c in steps
    ]

    for j in range(taps - 1):
        chan = tails_arg[j].astype(f32)
        matr = mtails_arg[j].astype(f32)
        for l in range(layers):
            i = l * (taps - 1) + j
            mtails_ref[i : i + 1, :] = matr[l : l + 1]
            for h in range(heads_n):
                tails_ref[h, i : i + 1, :] = chan[l : l + 1, h * channels : (h + 1) * channels]
    for q in range(seq_n):
        hidden_ref[q] = hidden_arg[q].astype(f32)
    dest = [group_ref[m] for m in range(members)]
    one, zero = jnp.int32(1), jnp.int32(0)
    rank = []
    for m in range(members):
        count = zero
        for e in range(m):
            count = count + jnp.where(dest[e] == dest[m], one, zero)
        rank.append(count)
    for m in range(members):
        row = dest[m] * capacity + s_me * pair + rank[m]
        rows_ref[m : m + 1, :] = jnp.full((1, 128), row, jnp.int32).astype(f32)
    source, keep = [], []
    for slot in range(capacity):
        at, found = zero, zero
        for m in range(members):
            hit = dest[m] * pair + rank[m] == slot
            at = at + jnp.where(hit, jnp.int32(m), zero)
            found = found + jnp.where(hit, one, zero)
        source.append(at)
        keep.append(found)

    barrier = pltpu.get_barrier_semaphore()

    @pl.loop(1, devices)
    def _(offset):
        s_to, h_to = peer(offset)
        pl.semaphore_signal(
            barrier, inc=1, device_id={"seq": s_to, "heads": h_to}, device_id_type=MESH
        )

    pl.semaphore_wait(barrier, devices - 1)

    pending = []

    def remote(src, dst, ssem, rsem, where):
        copy = pltpu.make_async_remote_copy(
            src_ref=src,
            dst_ref=dst,
            send_sem=ssem,
            recv_sem=rsem,
            device_id=where,
            device_id_type=MESH,
        )
        copy.start()
        pending.append(copy)
        return copy

    def token_copy(offset):
        s_to, h_to = peer(offset)
        return pltpu.make_async_remote_copy(
            src_ref=hidden_ref.at[s_to],
            dst_ref=hid_in.at[me],
            send_sem=tok_ssem.at[offset],
            recv_sem=tok_rsem.at[offset],
            device_id={"seq": s_to, "heads": h_to},
            device_id_type=MESH,
        )

    @pl.loop(1, devices)
    def _(offset):
        token_copy(offset).start()

    row_copies = [
        remote(
            rows_ref,
            rows_in.at[s_me],
            row_ssem.at[d],
            row_rsem.at[d],
            {"seq": lax.rem(s_me + d, seq_n)},
        )
        for d in range(1, seq_n)
    ]
    tail_copies = []
    for d in range(1, heads_n):
        h_to = lax.rem(h_me + d, heads_n)
        tail_copies.append(
            remote(
                tails_ref.at[h_to],
                tails_in.at[h_me],
                tail_ssem.at[d],
                tail_rsem.at[d],
                {"heads": h_to},
            )
        )
        tail_copies.append(
            remote(
                mtails_ref, mtails_in.at[h_me], mt_ssem.at[d], mt_rsem.at[d], {"heads": h_to}
            )
        )

    def send_state(step):
        l, c = steps[step]
        copies = []
        for d in range(1, heads_n):
            h_to = lax.rem(h_me + d, heads_n)
            copies.append(
                remote(
                    state_hbm.at[l, 0, 0, pl.ds(h_to * head_dev + c * group_heads, group_heads)],
                    state[l][c].at[h_me],
                    state_ssem.at[step, d],
                    state_rsem.at[step, d],
                    {"heads": h_to},
                )
            )
        return copies

    ahead = 3
    state_copies = {i: send_state(i) for i in range(min(ahead, len(steps)))}
    out_copies = []
    pumped = [0]

    def pump(upto):
        while pumped[0] < min(upto, len(steps)):
            step = pumped[0]
            pumped[0] += 1
            l, c = steps[step]
            own_load[step].wait()
            for copy in state_copies[step]:
                copy.wait_recv()
            if step + ahead < len(steps):
                state_copies[step + ahead] = send_state(step + ahead)
            heads = pl.ds(c * group_heads, group_heads)
            for slot in range(capacity):
                outbox[l, c, slot // pair, slot % pair] = state[l][c][source[slot]]
            place = raw_hbm.at[l, 0, pl.ds(s_me * pair, pair), heads]
            for d in range(1, seq_n):
                s_to = lax.rem(s_me + d, seq_n)
                out_copies.append(
                    remote(
                        outbox.at[l, c, s_to],
                        place,
                        out_ssem.at[step, d],
                        out_rsem.at[step, d],
                        {"seq": s_to},
                    )
                )
            own = pltpu.make_async_copy(
                outbox.at[l, c, s_me], place, local_sem.at[2 * layers + 2 + len(steps) + step]
            )
            own.start()
            loads.append(own)

    hid_in[me] = hidden_ref[s_me]
    rows_in[s_me] = rows_ref[...]
    tails_in[h_me] = tails_ref[h_me]
    mtails_in[h_me] = mtails_ref[...]

    @pl.loop(1, devices)
    def _(offset):
        token_copy(offset).wait_recv()

    for r in range(requests):
        current[r // chunk_rows, r % chunk_rows : r % chunk_rows + 1, :] = hid_in[r]

    even = lax.broadcasted_iota(jnp.int32, (128, 256), 1) - 2 * lax.broadcasted_iota(
        jnp.int32, (128, 256), 0
    )
    pick = [(even == 0).astype(bf16), (even == 1).astype(bf16)]
    expand = lax.broadcasted_iota(jnp.int32, (head_dev, channels), 1) - head_width * (
        lax.broadcasted_iota(jnp.int32, (head_dev, channels), 0)
    )
    expand = ((expand >= 0) & (expand < head_width)).astype(f32)

    def per_channel(values):
        return jnp.dot(
            values, expand, precision=lax.Precision.HIGHEST, preferred_element_type=f32
        )

    block = 256 if channels % 256 == 0 else channels
    block_out = 256 if width % 256 == 0 else width
    for l in range(layers):
        hidden = jnp.concatenate([current[c] for c in range(heads_n)], axis=0).astype(bf16)
        for k in range(width // 128):
            part_h = hidden[:, k * 128 : (k + 1) * 128]
            for half in range(2):
                spread[half * requests : (half + 1) * requests, k * 256 : (k + 1) * 256] = jnp.dot(
                    part_h, pick[half], preferred_element_type=f32
                ).astype(bf16)
        win_load[l].wait()
        weight = win.at[l].reshape(2 * width, channels)
        if block == channels:
            zx[...] = jnp.dot(spread[...], weight[...], preferred_element_type=f32)
        else:

            @pl.loop(0, channels // block)
            def _(n):
                cols = pl.ds(pl.multiple_of(n * block, block), block)
                zx[:, cols] = jnp.dot(spread[...], weight[:, cols], preferred_element_type=f32)

        if l == 0:
            wstep_load.wait()
            wmat_load.wait()
        step_part = lax.dot_general(
            hidden, wstep[l], (((1,), (1,)), ((), ())), preferred_element_type=f32
        )
        mat_part = jnp.dot(hidden, wmat[l], preferred_element_type=f32)
        for q in range(seq_n):
            rows = slice(q * members, (q + 1) * members)
            zx_send[l, q, 0] = zx[q * members : (q + 1) * members, :]
            zx_send[l, q, 1] = zx[requests + q * members : requests + (q + 1) * members, :]
            sm_send[l, q, :, 0:256] = mat_part[rows]
            sm_send[l, q, :, 256 : 256 + head_dev] = step_part[rows]
        copies = []
        for d in range(1, seq_n):
            s_to = lax.rem(s_me + d, seq_n)
            copies.append(
                remote(
                    zx_send.at[l, s_to],
                    zx_recv.at[l, d],
                    zx_ssem.at[l, d],
                    zx_rsem.at[l, d],
                    {"seq": s_to},
                )
            )
            copies.append(
                remote(
                    sm_send.at[l, s_to],
                    sm_recv.at[l, d],
                    sm_ssem.at[l, d],
                    sm_rsem.at[l, d],
                    {"seq": s_to},
                )
            )
        pump(l * chunks + (2 if l == 0 else chunks - 1))
        if l == 0:
            for copy in tail_copies + row_copies:
                copy.wait_recv()
            for m in range(members):
                for i in range(layers * (taps - 1)):
                    tails_rows[i, m : m + 1, :] = tails_in[m, i : i + 1, :]
                    mtails_rows[i, m : m + 1, :] = mtails_in[m, i : i + 1, :]
        for copy in copies:
            copy.wait_recv()
        zx_sum = zx_send[l, s_me]
        sm_sum = sm_send[l, s_me]
        for d in range(1, seq_n):
            zx_sum = zx_sum + zx_recv[l, d]
            sm_sum = sm_sum + sm_recv[l, d]
        gate = zx_sum[0]
        conv_x = cconv_ref[l, taps - 1 : taps, :] * zx_sum[1]
        conv_m = mconv_ref[l, taps - 1 : taps, :] * sm_sum[:, 0:256]
        for j in range(taps - 1):
            conv_x = conv_x + cconv_ref[l, j : j + 1, :] * tails_rows[l * (taps - 1) + j]
            conv_m = conv_m + mconv_ref[l, j : j + 1, :] * mtails_rows[l * (taps - 1) + j]
        conv_x = silu(conv_x)
        conv_m = silu(conv_m)
        half_m = conv_m.shape[1] // 2
        step_in = sm_sum[:, 256 : 256 + head_dev] + sbias_ref[l : l + 1, :]
        step = jnp.maximum(step_in, 0.0) + jnp.log1p(jnp.exp(-jnp.abs(step_in)))
        decay = jnp.exp(-jnp.exp(dlog_ref[l : l + 1, :]) * step)
        decay_ch = per_channel(decay)
        fresh_ch = per_channel(step) * conv_x
        skip = per_channel(jnp.broadcast_to(skip_ref[l : l + 1, :], (8, head_dev)))[0:1]
        in_m, out_m = conv_m[:, 0:half_m], conv_m[:, half_m:]
        for m in range(members):
            vec_rows[l, m, 0:1, :] = decay_ch[m : m + 1]
            vec_rows[l, m, 1:2, :] = fresh_ch[m : m + 1]
            vec_rows[l, m, 2:3, 0:half_m] = in_m[m : m + 1]

        pump((l + 1) * chunks)
        lane = lax.broadcasted_iota(jnp.int32, (group_rows, 128), 1)
        for c in range(chunks):
            total = jnp.zeros((group_rows, 128), f32)
            for m in range(members):
                old = state[l][c][m].reshape(group_rows, half_m).astype(f32)
                read = jnp.sum(old * out_m[m : m + 1], axis=1, keepdims=True)
                total = jnp.where(lane == m, read, total)
            col_y[c * group_rows : (c + 1) * group_rows, :] = total

        for k in range(channels_pad // 128):
            cols = slice(k * 128, (k + 1) * 128)
            flip_a[:, cols] = col_y[cols, :].T
        both = jnp.sum(in_m * out_m, axis=1, keepdims=True)
        read_out = decay_ch * flip_a[0:members, 0:channels] + fresh_ch * both
        gated = (read_out + skip * conv_x) * silu(gate)
        gated_send[l] = gated
        gated_all[l, s_me] = gated
        square = jnp.broadcast_to(jnp.sum(gated * gated, axis=1, keepdims=True), (members, 128))
        ss_all[l, me] = square
        g_copies = []
        for d in range(1, seq_n):
            g_copies.append(
                remote(
                    gated_send.at[l],
                    gated_all.at[l, s_me],
                    g_ssem.at[l, d],
                    g_rsem.at[l, d],
                    {"seq": lax.rem(s_me + d, seq_n)},
                )
            )

        def square_copy(offset):
            s_to, h_to = peer(offset)
            return pltpu.make_async_remote_copy(
                src_ref=ss_all.at[l, me],
                dst_ref=ss_all.at[l, me],
                send_sem=ss_ssem.at[l, offset],
                recv_sem=ss_rsem.at[l, offset],
                device_id={"seq": s_to, "heads": h_to},
                device_id_type=MESH,
            )

        @pl.loop(1, devices)
        def _(offset):
            square_copy(offset).start()

        for slot in range(capacity):
            vec_send[l, slot // pair, slot % pair] = vec_rows[l, source[slot]] * keep[slot].astype(
                f32
            )
        for d in range(1, seq_n):
            s_to = lax.rem(s_me + d, seq_n)
            out_copies.append(
                remote(
                    vec_send.at[l, s_to],
                    vec_hbm.at[l, pl.ds(s_me * pair, pair)],
                    vec_ssem.at[l, d],
                    vec_rsem.at[l, d],
                    {"seq": s_to},
                )
            )
        own = pltpu.make_async_copy(
            vec_send.at[l, s_me],
            vec_hbm.at[l, pl.ds(s_me * pair, pair)],
            local_sem.at[2 * layers + 2 + 2 * len(steps) + l],
        )
        own.start()
        loads.append(own)

        if l + 1 < layers:
            pump((l + 1) * chunks + 1)

        for copy in g_copies:
            copy.wait_recv()

        @pl.loop(1, devices)
        def _(offset):
            square_copy(offset).wait()

        for q in range(seq_n):
            total_sq = ss_all[l, q * heads_n]
            for h in range(1, heads_n):
                total_sq = total_sq + ss_all[l, q * heads_n + h]
            scale = lax.rsqrt(total_sq[:, 0:1] / model_width + epsilon)
            normed_ref[q * members : (q + 1) * members, :] = (
                gated_all[l, q] * scale * ngain_ref[l : l + 1, :]
            )
        wout_load[l].wait()
        normed = normed_ref[...].astype(bf16)
        if block_out == width:
            zout = jnp.dot(normed, wout[l], preferred_element_type=f32)
            for c in range(heads_n):
                part[l, c] = zout[c * chunk_rows : (c + 1) * chunk_rows]
        else:

            @pl.loop(0, width // block_out)
            def _(n):
                cols = pl.ds(pl.multiple_of(n * block_out, block_out), block_out)
                zout = jnp.dot(normed, wout[l, :, cols], preferred_element_type=f32)
                for c in range(heads_n):
                    part[l, c, :, cols] = zout[c * chunk_rows : (c + 1) * chunk_rows]

        copies = []
        for d in range(1, heads_n):
            h_to = lax.rem(h_me + d, heads_n)
            copies.append(
                remote(
                    part.at[l, h_to],
                    part_recv.at[l, d],
                    part_ssem.at[l, d],
                    part_rsem.at[l, d],
                    {"heads": h_to},
                )
            )
        for copy in copies:
            copy.wait_recv()
        summed = part[l, h_me]
        for d in range(1, heads_n):
            summed = summed + part_recv[l, d]
        base = current if l == 0 else result_send.at[l - 1]
        result_send[l, h_me] = (base[h_me] + summed).astype(bf16).astype(f32)
        copies = []
        for d in range(1, heads_n):
            h_to = lax.rem(h_me + d, heads_n)
            copies.append(
                remote(
                    result_send.at[l, h_me],
                    result_send.at[l, h_me],
                    res_ssem.at[l, d],
                    res_rsem.at[l, d],
                    {"heads": h_to},
                )
            )
        for copy in copies:
            copy.wait_recv()
        current_next = result_send.at[l]
        if l + 1 < layers:
            for c in range(heads_n):
                current[c] = current_next[c]
            pump((l + 1) * chunks + chunks // 2)

    final = jnp.concatenate([result_send[layers - 1, c] for c in range(heads_n)], axis=0)
    targets = jnp.concatenate([rows_in[q] for q in range(seq_n)], axis=0)
    wanted = (h_me * share_rows).astype(f32) + lax.broadcasted_iota(
        jnp.int32, (requests, 128), 1
    ).astype(f32)
    hot = (targets == wanted).astype(f32).astype(bf16)
    chosen = lax.dot_general(
        hot, final.astype(bf16), (((0,), (0,)), ((), ())), preferred_element_type=f32
    )
    decoded_ref[...] = chosen[0:share_rows].astype(bf16)

    @pl.loop(1, devices)
    def _(offset):
        token_copy(offset).wait_send()

    for copy in loads:
        copy.wait()
    for copy in pending:
        copy.wait_send()
    for copy in out_copies:
        copy.wait_recv()


def update_kernel(dims, vec_ref, raw_ref, given_ref, new_ref, decoded_ref, flip, cols):
    capacity, group_rows, state_width, channels = dims
    at = pl.program_id(1)

    @pl.when(at == 0)
    def _():
        decoded_ref[...] = given_ref[...]
        for r in range(capacity):
            flip[r : r + 1, 0:channels] = vec_ref[0, r, 0:1, :]
            flip[capacity + r : capacity + r + 1, 0:channels] = vec_ref[0, r, 1:2, :]
        for k in range(flip.shape[1] // 128):
            part = slice(k * 128, (k + 1) * 128)
            cols[part, :] = flip[:, part].T

    rows = pl.ds(pl.multiple_of(at * group_rows, 8), group_rows)
    for r in range(capacity):
        old = raw_ref[0, 0, r].reshape(group_rows, state_width).astype(f32)
        fresh = cols[rows, r : r + 1] * old + (
            cols[rows, capacity + r : capacity + r + 1] * vec_ref[0, r, 2:3, 0:state_width]
        )
        new_ref[0, 0, r] = fresh.astype(bf16).reshape(new_ref.shape[3:])


def on_device(
    final_state,
    channel_tail,
    matrix_tail,
    last_hidden,
    decode_group,
    input_weight,
    step_weight,
    matrix_weight,
    channel_conv,
    matrix_conv,
    step_bias,
    decay_log,
    skip_gain,
    norm_gain,
    output_weight,
):
    heads_n = lax.axis_size("heads")
    seq_n = lax.axis_size("seq")
    layers, _, slots, heads_all, head_width, state_width = final_state.shape
    head_dev = heads_all // heads_n
    model_width = last_hidden.shape[2]
    width = model_width // seq_n
    taps = channel_conv.shape[1]
    members = heads_n * slots
    pair = 2 * members // seq_n
    capacity = seq_n * pair
    requests = seq_n * members
    share_rows = capacity * seq_n // heads_n
    chunk_rows = requests // heads_n
    channels = head_dev * head_width
    channels_pad = -(-channels // 128) * 128
    tail_rows = layers * (taps - 1)
    devices = seq_n * heads_n

    group_heads = 4 if head_dev % 4 == 0 else head_dev
    chunks = head_dev // group_heads
    steps = layers * chunks
    groups = decode_group.reshape(members)
    tails = jnp.transpose(channel_tail.reshape(layers, taps - 1, model_width), (1, 0, 2))
    mtails = jnp.transpose(matrix_tail.reshape(layers, taps - 1, 2 * state_width), (1, 0, 2))
    hidden = last_hidden.reshape(seq_n, 1, width)

    dims = (
        layers, heads_n, seq_n, members, head_dev, head_width, width, channels, pair, taps
    )
    vmem = pl.BlockSpec(memory_space=pltpu.VMEM)
    smem = pl.BlockSpec(memory_space=pltpu.SMEM)
    anyw = pl.BlockSpec(memory_space=pl.ANY)
    V = pltpu.VMEM
    dma = pltpu.SemaphoreType.DMA
    scratch = [
        V((layers, width, 2, channels), bf16),
        V((layers, channels, width), bf16),
        V((layers, head_dev, width), bf16),
        V((layers, width, 2 * state_width), bf16),
        V((layers, chunks, seq_n, pair, group_heads, head_width, state_width), bf16),
        V((requests, 1, width), f32),
        V((heads_n, tail_rows, channels), f32),
        V((heads_n, tail_rows, 2 * state_width), f32),
        V((seq_n, members, 128), f32),
        V((tail_rows, members, channels), f32),
        V((tail_rows, members, 2 * state_width), f32),
        V((heads_n, chunk_rows, width), f32),
        V((2 * requests, 2 * width), bf16),
        V((2 * requests, channels), f32),
        V((layers, seq_n, 2, members, channels), f32),
        V((layers, seq_n, 2, members, channels), f32),
        V((layers, seq_n, members, 384), f32),
        V((layers, seq_n, members, 384), f32),
        V((128, channels_pad), f32),
        V((channels_pad, 128), f32),
        V((heads_n, tail_rows, channels), f32),
        V((tail_rows, 2 * state_width), f32),
        V((seq_n, 1, width), f32),
        V((members, 128), f32),
        V((layers, members, 3, channels), f32),
        V((layers, seq_n, pair, 3, channels), f32),
        V((layers, seq_n, members, channels), f32),
        V((layers, members, channels), f32),
        V((layers, devices, members, 128), f32),
        V((requests, channels), f32),
        V((layers, heads_n, chunk_rows, width), f32),
        V((layers, heads_n, chunk_rows, width), f32),
        V((layers, heads_n, chunk_rows, width), f32),
        dma((3 * layers + 2 + 2 * steps,)),
        dma((steps, heads_n)),
        dma((steps, heads_n)),
        dma((devices,)),
        dma((devices,)),
        dma((seq_n,)),
        dma((seq_n,)),
        dma((heads_n,)),
        dma((heads_n,)),
        dma((heads_n,)),
        dma((heads_n,)),
        dma((layers, seq_n)),
        dma((layers, seq_n)),
        dma((layers, seq_n)),
        dma((layers, seq_n)),
        dma((layers, seq_n)),
        dma((layers, seq_n)),
        dma((layers, devices)),
        dma((layers, devices)),
        dma((layers, heads_n)),
        dma((layers, heads_n)),
        dma((layers, heads_n)),
        dma((layers, heads_n)),
        dma((steps, seq_n)),
        dma((steps, seq_n)),
        dma((layers, seq_n)),
        dma((layers, seq_n)),
    ] + [V((members, group_heads, head_width, state_width), bf16) for _ in range(steps)]
    decoded, raw, vectors = pl.pallas_call(
        functools.partial(kernel, dims),
        out_shape=(
            jax.ShapeDtypeStruct((share_rows, width), bf16),
            jax.ShapeDtypeStruct(
                (layers, 1, capacity, head_dev, head_width, state_width), bf16
            ),
            jax.ShapeDtypeStruct((layers, capacity, 3, channels), f32),
        ),
        in_specs=[
            smem, anyw, vmem, vmem, vmem, anyw, anyw, anyw,
            vmem, vmem, vmem, vmem, vmem, vmem, anyw,
        ],
        out_specs=(vmem, anyw, anyw),
        scratch_shapes=scratch,
        compiler_params=pltpu.CompilerParams(
            collective_id=0, has_side_effects=True, vmem_limit_bytes=58 * 1024 * 1024
        ),
        cost_estimate=pl.CostEstimate(
            flops=4 * requests * width * channels * 3 * layers,
            bytes_accessed=30_000_000,
            transcendentals=0,
        ),
        name="handover",
    )(
        groups,
        final_state,
        tails,
        mtails,
        hidden,
        input_weight,
        jnp.swapaxes(step_weight, 1, 2),
        matrix_weight,
        channel_conv,
        matrix_conv,
        step_bias,
        decay_log,
        skip_gain,
        norm_gain,
        output_weight,
    )
    block = (1, 1, capacity, group_heads, head_width, state_width)
    new_state, decoded = pl.pallas_call(
        functools.partial(
            update_kernel, (capacity, group_heads * head_width, state_width, channels)
        ),
        grid=(layers, chunks),
        out_shape=(
            jax.ShapeDtypeStruct(raw.shape, bf16),
            jax.ShapeDtypeStruct(decoded.shape, bf16),
        ),
        in_specs=[
            pl.BlockSpec((1, capacity, 3, channels), lambda l, c: (l, 0, 0, 0)),
            pl.BlockSpec(block, lambda l, c: (l, 0, 0, c, 0, 0)),
            pl.BlockSpec((share_rows, width), lambda l, c: (0, 0)),
        ],
        out_specs=(
            pl.BlockSpec(block, lambda l, c: (l, 0, 0, c, 0, 0)),
            pl.BlockSpec((share_rows, width), lambda l, c: (0, 0)),
        ),
        scratch_shapes=[V((128, channels_pad), f32), V((channels_pad, 128), f32)],
        compiler_params=pltpu.CompilerParams(vmem_limit_bytes=32 * 1024 * 1024),
        name="update",
    )(vectors, raw, decoded)
    return decoded, new_state


def solution(mesh):
    return jax.shard_map(
        on_device,
        mesh=mesh,
        in_specs=(
            P(None, ("groups", "seq", "heads"), None, None, None, None),
            P(None, ("groups", "seq", "heads"), None, None, None),
            P(("groups", "seq", "heads"), None, None, None, None),
            P(("groups", "seq", "heads"), None, None),
            P(("groups", "seq"), None),
            P(None, "seq", None, "heads"),
            P(None, "seq", "heads"),
            P(None, "seq", None),
            P(None, None, "heads"),
            P(),
            P(None, "heads"),
            P(None, "heads"),
            P(None, "heads"),
            P(None, "heads"),
            P(None, "heads", "seq"),
        ),
        out_specs=(
            P(("groups", "heads"), "seq"),
            P(None, ("groups", "seq"), None, "heads", None, None),
        ),
        check_vma=False,
    )
```

```python
import functools

import jax
import jax.numpy as jnp
from jax import lax
from jax.experimental import pallas as pl
from jax.experimental.pallas import tpu as pltpu
from jax.sharding import PartitionSpec as P

epsilon = 1e-05
f32 = jnp.float32
bf16 = jnp.bfloat16
MESH = pl.DeviceIdType.MESH


def silu(v):
    return v / (1.0 + jnp.exp(-v))


def kernel(
    dims,
    group_ref,
    state_hbm,
    tails_arg,
    mtails_arg,
    hidden_arg,
    win_hbm,
    wstep_hbm,
    wmat_hbm,
    cconv_ref,
    mconv_ref,
    sbias_ref,
    dlog_ref,
    skip_ref,
    ngain_ref,
    wout_hbm,
    decoded_ref,
    raw_hbm,
    vec_hbm,
    win,
    wout,
    wstep,
    wmat,
    outbox,
    hid_in,
    tails_in,
    mtails_in,
    rows_in,
    tails_rows,
    mtails_rows,
    current,
    spread,
    zx,
    zx_send,
    zx_recv,
    sm_send,
    sm_recv,
    flip_a,
    col_y,
    tails_ref,
    mtails_ref,
    hidden_ref,
    rows_ref,
    vec_rows,
    vec_send,
    gated_all,
    gated_send,
    ss_all,
    normed_ref,
    part,
    part_recv,
    result_send,
    local_sem,
    state_ssem,
    state_rsem,
    tok_ssem,
    tok_rsem,
    row_ssem,
    row_rsem,
    tail_ssem,
    tail_rsem,
    mt_ssem,
    mt_rsem,
    zx_ssem,
    zx_rsem,
    sm_ssem,
    sm_rsem,
    g_ssem,
    g_rsem,
    ss_ssem,
    ss_rsem,
    part_ssem,
    part_rsem,
    res_ssem,
    res_rsem,
    out_ssem,
    out_rsem,
    vec_ssem,
    vec_rsem,
    *state_flat,
):
    layers, heads_n, seq_n, members, head_dev, head_width, width, channels, pair, taps = dims
    requests = seq_n * members
    chunk_rows = requests // heads_n
    share_rows = decoded_ref.shape[0]
    model_width = width * seq_n
    s_me = lax.axis_index("seq")
    h_me = lax.axis_index("heads")
    me = s_me * heads_n + h_me
    devices = seq_n * heads_n
    channels_pad = flip_a.shape[1]
    group_heads = 4 if head_dev % 4 == 0 else head_dev
    group_rows = group_heads * head_width
    chunks = head_dev // group_heads
    steps = [(l, c) for l in range(layers) for c in range(chunks)]
    state = [[state_flat[l * chunks + c] for c in range(chunks)] for l in range(layers)]
    capacity = seq_n * pair

    loads = []

    def load(src, dst, index):
        copy = pltpu.make_async_copy(src, dst, local_sem.at[index])
        copy.start()
        return copy

    def peer(offset):
        other = lax.rem(me + offset, devices)
        return other // heads_n, lax.rem(other, heads_n)

    win_load = [load(win_hbm.at[l], win.at[l], l) for l in range(layers)]
    wout_load = [load(wout_hbm.at[l], wout.at[l], layers + l) for l in range(layers)]
    wstep_load = load(wstep_hbm, wstep, 2 * layers)
    wmat_load = load(wmat_hbm, wmat, 2 * layers + 1)
    own_load = [
        load(
            state_hbm.at[l, 0, 0, pl.ds(h_me * head_dev + c * group_heads, group_heads)],
            state[l][c].at[h_me],
            2 * layers + 2 + l * chunks + c,
        )
        for l, c in steps
    ]

    for j in range(taps - 1):
        chan = tails_arg[j].astype(f32)
        matr = mtails_arg[j].astype(f32)
        for l in range(layers):
            i = l * (taps - 1) + j
            mtails_ref[i : i + 1, :] = matr[l : l + 1]
            for h in range(heads_n):
                tails_ref[h, i : i + 1, :] = chan[l : l + 1, h * channels : (h + 1) * channels]
    for q in range(seq_n):
        hidden_ref[q] = hidden_arg[q].astype(f32)
    dest = [group_ref[m] for m in range(members)]
    one, zero = jnp.int32(1), jnp.int32(0)
    rank = []
    for m in range(members):
        count = zero
        for e in range(m):
            count = count + jnp.where(dest[e] == dest[m], one, zero)
        rank.append(count)
    for m in range(members):
        row = dest[m] * capacity + s_me * pair + rank[m]
        rows_ref[m : m + 1, :] = jnp.full((1, 128), row, jnp.int32).astype(f32)
    source, keep = [], []
    for slot in range(capacity):
        at, found = zero, zero
        for m in range(members):
            hit = dest[m] * pair + rank[m] == slot
            at = at + jnp.where(hit, jnp.int32(m), zero)
            found = found + jnp.where(hit, one, zero)
        source.append(at)
        keep.append(found)

    barrier = pltpu.get_barrier_semaphore()

    @pl.loop(1, devices)
    def _(offset):
        s_to, h_to = peer(offset)
        pl.semaphore_signal(
            barrier, inc=1, device_id={"seq": s_to, "heads": h_to}, device_id_type=MESH
        )

    pl.semaphore_wait(barrier, devices - 1)

    pending = []

    def remote(src, dst, ssem, rsem, where):
        copy = pltpu.make_async_remote_copy(
            src_ref=src,
            dst_ref=dst,
            send_sem=ssem,
            recv_sem=rsem,
            device_id=where,
            device_id_type=MESH,
        )
        copy.start()
        pending.append(copy)
        return copy

    def token_copy(offset):
        s_to, h_to = peer(offset)
        return pltpu.make_async_remote_copy(
            src_ref=hidden_ref.at[s_to],
            dst_ref=hid_in.at[me],
            send_sem=tok_ssem.at[offset],
            recv_sem=tok_rsem.at[offset],
            device_id={"seq": s_to, "heads": h_to},
            device_id_type=MESH,
        )

    @pl.loop(1, devices)
    def _(offset):
        token_copy(offset).start()

    row_copies = [
        remote(
            rows_ref,
            rows_in.at[s_me],
            row_ssem.at[d],
            row_rsem.at[d],
            {"seq": lax.rem(s_me + d, seq_n)},
        )
        for d in range(1, seq_n)
    ]
    tail_copies = []
    for d in range(1, heads_n):
        h_to = lax.rem(h_me + d, heads_n)
        tail_copies.append(
            remote(
                tails_ref.at[h_to],
                tails_in.at[h_me],
                tail_ssem.at[d],
                tail_rsem.at[d],
                {"heads": h_to},
            )
        )
        tail_copies.append(
            remote(
                mtails_ref, mtails_in.at[h_me], mt_ssem.at[d], mt_rsem.at[d], {"heads": h_to}
            )
        )

    def send_state(step):
        l, c = steps[step]
        copies = []
        for d in range(1, heads_n):
            h_to = lax.rem(h_me + d, heads_n)
            copies.append(
                remote(
                    state_hbm.at[l, 0, 0, pl.ds(h_to * head_dev + c * group_heads, group_heads)],
                    state[l][c].at[h_me],
                    state_ssem.at[step, d],
                    state_rsem.at[step, d],
                    {"heads": h_to},
                )
            )
        return copies

    ahead = 2
    state_copies = {i: send_state(i) for i in range(min(ahead, len(steps)))}
    out_copies = []
    pumped = [0]

    def pump(upto):
        while pumped[0] < min(upto, len(steps)):
            step = pumped[0]
            pumped[0] += 1
            l, c = steps[step]
            own_load[step].wait()
            for copy in state_copies[step]:
                copy.wait_recv()
            if step + ahead < len(steps):
                state_copies[step + ahead] = send_state(step + ahead)
            heads = pl.ds(c * group_heads, group_heads)
            for slot in range(capacity):
                outbox[l, c, slot // pair, slot % pair] = state[l][c][source[slot]]
            place = raw_hbm.at[l, 0, pl.ds(s_me * pair, pair), heads]
            for d in range(1, seq_n):
                s_to = lax.rem(s_me + d, seq_n)
                out_copies.append(
                    remote(
                        outbox.at[l, c, s_to],
                        place,
                        out_ssem.at[step, d],
                        out_rsem.at[step, d],
                        {"seq": s_to},
                    )
                )
            own = pltpu.make_async_copy(
                outbox.at[l, c, s_me], place, local_sem.at[2 * layers + 2 + len(steps) + step]
            )
            own.start()
            loads.append(own)

    hid_in[me] = hidden_ref[s_me]
    rows_in[s_me] = rows_ref[...]
    tails_in[h_me] = tails_ref[h_me]
    mtails_in[h_me] = mtails_ref[...]

    @pl.loop(1, devices)
    def _(offset):
        token_copy(offset).wait_recv()

    for r in range(requests):
        current[r // chunk_rows, r % chunk_rows : r % chunk_rows + 1, :] = hid_in[r]

    even = lax.broadcasted_iota(jnp.int32, (128, 256), 1) - 2 * lax.broadcasted_iota(
        jnp.int32, (128, 256), 0
    )
    pick = [(even == 0).astype(bf16), (even == 1).astype(bf16)]
    expand = lax.broadcasted_iota(jnp.int32, (head_dev, channels), 1) - head_width * (
        lax.broadcasted_iota(jnp.int32, (head_dev, channels), 0)
    )
    expand = ((expand >= 0) & (expand < head_width)).astype(f32)

    def per_channel(values):
        return jnp.dot(
            values, expand, precision=lax.Precision.HIGHEST, preferred_element_type=f32
        )

    block = 256 if channels % 256 == 0 else channels
    block_out = 256 if width % 256 == 0 else width
    for l in range(layers):
        hidden = jnp.concatenate([current[c] for c in range(heads_n)], axis=0).astype(bf16)
        for k in range(width // 128):
            part_h = hidden[:, k * 128 : (k + 1) * 128]
            for half in range(2):
                spread[half * requests : (half + 1) * requests, k * 256 : (k + 1) * 256] = jnp.dot(
                    part_h, pick[half], preferred_element_type=f32
                ).astype(bf16)
        win_load[l].wait()
        weight = win.at[l].reshape(2 * width, channels)
        if block == channels:
            zx[...] = jnp.dot(spread[...], weight[...], preferred_element_type=f32)
        else:

            @pl.loop(0, channels // block)
            def _(n):
                cols = pl.ds(pl.multiple_of(n * block, block), block)
                zx[:, cols] = jnp.dot(spread[...], weight[:, cols], preferred_element_type=f32)

        if l == 0:
            wstep_load.wait()
            wmat_load.wait()
        step_part = lax.dot_general(
            hidden, wstep[l], (((1,), (1,)), ((), ())), preferred_element_type=f32
        )
        mat_part = jnp.dot(hidden, wmat[l], preferred_element_type=f32)
        for q in range(seq_n):
            rows = slice(q * members, (q + 1) * members)
            zx_send[l, q, 0] = zx[q * members : (q + 1) * members, :]
            zx_send[l, q, 1] = zx[requests + q * members : requests + (q + 1) * members, :]
            sm_send[l, q, :, 0:256] = mat_part[rows]
            sm_send[l, q, :, 256 : 256 + head_dev] = step_part[rows]
        copies = []
        for d in range(1, seq_n):
            s_to = lax.rem(s_me + d, seq_n)
            copies.append(
                remote(
                    zx_send.at[l, s_to],
                    zx_recv.at[l, d],
                    zx_ssem.at[l, d],
                    zx_rsem.at[l, d],
                    {"seq": s_to},
                )
            )
            copies.append(
                remote(
                    sm_send.at[l, s_to],
                    sm_recv.at[l, d],
                    sm_ssem.at[l, d],
                    sm_rsem.at[l, d],
                    {"seq": s_to},
                )
            )
        pump(2 if l == 0 else (l + 1) * chunks)
        if l == 0:
            for copy in tail_copies + row_copies:
                copy.wait_recv()
            for m in range(members):
                for i in range(layers * (taps - 1)):
                    tails_rows[i, m : m + 1, :] = tails_in[m, i : i + 1, :]
                    mtails_rows[i, m : m + 1, :] = mtails_in[m, i : i + 1, :]
        for copy in copies:
            copy.wait_recv()
        zx_sum = zx_send[l, s_me]
        sm_sum = sm_send[l, s_me]
        for d in range(1, seq_n):
            zx_sum = zx_sum + zx_recv[l, d]
            sm_sum = sm_sum + sm_recv[l, d]
        gate = zx_sum[0]
        conv_x = cconv_ref[l, taps - 1 : taps, :] * zx_sum[1]
        conv_m = mconv_ref[l, taps - 1 : taps, :] * sm_sum[:, 0:256]
        for j in range(taps - 1):
            conv_x = conv_x + cconv_ref[l, j : j + 1, :] * tails_rows[l * (taps - 1) + j]
            conv_m = conv_m + mconv_ref[l, j : j + 1, :] * mtails_rows[l * (taps - 1) + j]
        conv_x = silu(conv_x)
        conv_m = silu(conv_m)
        half_m = conv_m.shape[1] // 2
        step_in = sm_sum[:, 256 : 256 + head_dev] + sbias_ref[l : l + 1, :]
        step = jnp.maximum(step_in, 0.0) + jnp.log1p(jnp.exp(-jnp.abs(step_in)))
        decay = jnp.exp(-jnp.exp(dlog_ref[l : l + 1, :]) * step)
        decay_ch = per_channel(decay)
        fresh_ch = per_channel(step) * conv_x
        skip = per_channel(jnp.broadcast_to(skip_ref[l : l + 1, :], (8, head_dev)))[0:1]
        in_m, out_m = conv_m[:, 0:half_m], conv_m[:, half_m:]
        for m in range(members):
            vec_rows[l, m, 0:1, :] = decay_ch[m : m + 1]
            vec_rows[l, m, 1:2, :] = fresh_ch[m : m + 1]
            vec_rows[l, m, 2:3, 0:half_m] = in_m[m : m + 1]

        pump((l + 1) * chunks)
        lane = lax.broadcasted_iota(jnp.int32, (group_rows, 128), 1)
        for c in range(chunks):
            total = jnp.zeros((group_rows, 128), f32)
            for m in range(members):
                old = state[l][c][m].reshape(group_rows, half_m).astype(f32)
                read = jnp.sum(old * out_m[m : m + 1], axis=1, keepdims=True)
                total = jnp.where(lane == m, read, total)
            col_y[c * group_rows : (c + 1) * group_rows, :] = total

        for k in range(channels_pad // 128):
            cols = slice(k * 128, (k + 1) * 128)
            flip_a[:, cols] = col_y[cols, :].T
        both = jnp.sum(in_m * out_m, axis=1, keepdims=True)
        read_out = decay_ch * flip_a[0:members, 0:channels] + fresh_ch * both
        gated = (read_out + skip * conv_x) * silu(gate)
        gated_send[l] = gated
        gated_all[l, s_me] = gated
        square = jnp.broadcast_to(jnp.sum(gated * gated, axis=1, keepdims=True), (members, 128))
        ss_all[l, me] = square
        g_copies = []
        for d in range(1, seq_n):
            g_copies.append(
                remote(
                    gated_send.at[l],
                    gated_all.at[l, s_me],
                    g_ssem.at[l, d],
                    g_rsem.at[l, d],
                    {"seq": lax.rem(s_me + d, seq_n)},
                )
            )

        def square_copy(offset):
            s_to, h_to = peer(offset)
            return pltpu.make_async_remote_copy(
                src_ref=ss_all.at[l, me],
                dst_ref=ss_all.at[l, me],
                send_sem=ss_ssem.at[l, offset],
                recv_sem=ss_rsem.at[l, offset],
                device_id={"seq": s_to, "heads": h_to},
                device_id_type=MESH,
            )

        @pl.loop(1, devices)
        def _(offset):
            square_copy(offset).start()

        for slot in range(capacity):
            vec_send[l, slot // pair, slot % pair] = vec_rows[l, source[slot]] * keep[slot].astype(
                f32
            )
        for d in range(1, seq_n):
            s_to = lax.rem(s_me + d, seq_n)
            out_copies.append(
                remote(
                    vec_send.at[l, s_to],
                    vec_hbm.at[l, pl.ds(s_me * pair, pair)],
                    vec_ssem.at[l, d],
                    vec_rsem.at[l, d],
                    {"seq": s_to},
                )
            )
        own = pltpu.make_async_copy(
            vec_send.at[l, s_me],
            vec_hbm.at[l, pl.ds(s_me * pair, pair)],
            local_sem.at[2 * layers + 2 + 2 * len(steps) + l],
        )
        own.start()
        loads.append(own)

        if l + 1 < layers:
            pump((l + 1) * chunks + 2)

        for copy in g_copies:
            copy.wait_recv()

        @pl.loop(1, devices)
        def _(offset):
            square_copy(offset).wait()

        for q in range(seq_n):
            total_sq = ss_all[l, q * heads_n]
            for h in range(1, heads_n):
                total_sq = total_sq + ss_all[l, q * heads_n + h]
            scale = lax.rsqrt(total_sq[:, 0:1] / model_width + epsilon)
            normed_ref[q * members : (q + 1) * members, :] = (
                gated_all[l, q] * scale * ngain_ref[l : l + 1, :]
            )
        wout_load[l].wait()
        normed = normed_ref[...].astype(bf16)
        if block_out == width:
            zout = jnp.dot(normed, wout[l], preferred_element_type=f32)
            for c in range(heads_n):
                part[l, c] = zout[c * chunk_rows : (c + 1) * chunk_rows]
        else:

            @pl.loop(0, width // block_out)
            def _(n):
                cols = pl.ds(pl.multiple_of(n * block_out, block_out), block_out)
                zout = jnp.dot(normed, wout[l, :, cols], preferred_element_type=f32)
                for c in range(heads_n):
                    part[l, c, :, cols] = zout[c * chunk_rows : (c + 1) * chunk_rows]

        copies = []
        for d in range(1, heads_n):
            h_to = lax.rem(h_me + d, heads_n)
            copies.append(
                remote(
                    part.at[l, h_to],
                    part_recv.at[l, d],
                    part_ssem.at[l, d],
                    part_rsem.at[l, d],
                    {"heads": h_to},
                )
            )
        for copy in copies:
            copy.wait_recv()
        summed = part[l, h_me]
        for d in range(1, heads_n):
            summed = summed + part_recv[l, d]
        base = current if l == 0 else result_send.at[l - 1]
        result_send[l, h_me] = (base[h_me] + summed).astype(bf16).astype(f32)
        copies = []
        for d in range(1, heads_n):
            h_to = lax.rem(h_me + d, heads_n)
            copies.append(
                remote(
                    result_send.at[l, h_me],
                    result_send.at[l, h_me],
                    res_ssem.at[l, d],
                    res_rsem.at[l, d],
                    {"heads": h_to},
                )
            )
        for copy in copies:
            copy.wait_recv()
        current_next = result_send.at[l]
        if l + 1 < layers:
            for c in range(heads_n):
                current[c] = current_next[c]
            pump((l + 1) * chunks + chunks - 1)

    final = jnp.concatenate([result_send[layers - 1, c] for c in range(heads_n)], axis=0)
    targets = jnp.concatenate([rows_in[q] for q in range(seq_n)], axis=0)
    wanted = (h_me * share_rows).astype(f32) + lax.broadcasted_iota(
        jnp.int32, (requests, 128), 1
    ).astype(f32)
    hot = (targets == wanted).astype(f32).astype(bf16)
    chosen = lax.dot_general(
        hot, final.astype(bf16), (((0,), (0,)), ((), ())), preferred_element_type=f32
    )
    decoded_ref[...] = chosen[0:share_rows].astype(bf16)

    @pl.loop(1, devices)
    def _(offset):
        token_copy(offset).wait_send()

    for copy in loads:
        copy.wait()
    for copy in pending:
        copy.wait_send()
    for copy in out_copies:
        copy.wait_recv()


def update_kernel(dims, vec_ref, raw_ref, given_ref, new_ref, decoded_ref, flip, cols):
    capacity, group_rows, state_width, channels = dims
    at = pl.program_id(1)

    @pl.when(at == 0)
    def _():
        decoded_ref[...] = given_ref[...]
        for r in range(capacity):
            flip[r : r + 1, 0:channels] = vec_ref[0, r, 0:1, :]
            flip[capacity + r : capacity + r + 1, 0:channels] = vec_ref[0, r, 1:2, :]
        for k in range(flip.shape[1] // 128):
            part = slice(k * 128, (k + 1) * 128)
            cols[part, :] = flip[:, part].T

    rows = pl.ds(pl.multiple_of(at * group_rows, 8), group_rows)
    for r in range(capacity):
        old = raw_ref[0, 0, r].reshape(group_rows, state_width).astype(f32)
        fresh = cols[rows, r : r + 1] * old + (
            cols[rows, capacity + r : capacity + r + 1] * vec_ref[0, r, 2:3, 0:state_width]
        )
        new_ref[0, 0, r] = fresh.astype(bf16).reshape(new_ref.shape[3:])


def on_device(
    final_state,
    channel_tail,
    matrix_tail,
    last_hidden,
    decode_group,
    input_weight,
    step_weight,
    matrix_weight,
    channel_conv,
    matrix_conv,
    step_bias,
    decay_log,
    skip_gain,
    norm_gain,
    output_weight,
):
    heads_n = lax.axis_size("heads")
    seq_n = lax.axis_size("seq")
    layers, _, slots, heads_all, head_width, state_width = final_state.shape
    head_dev = heads_all // heads_n
    model_width = last_hidden.shape[2]
    width = model_width // seq_n
    taps = channel_conv.shape[1]
    members = heads_n * slots
    pair = 2 * members // seq_n
    capacity = seq_n * pair
    requests = seq_n * members
    share_rows = capacity * seq_n // heads_n
    chunk_rows = requests // heads_n
    channels = head_dev * head_width
    channels_pad = -(-channels // 128) * 128
    tail_rows = layers * (taps - 1)
    devices = seq_n * heads_n

    group_heads = 4 if head_dev % 4 == 0 else head_dev
    chunks = head_dev // group_heads
    steps = layers * chunks
    groups = decode_group.reshape(members)
    tails = jnp.transpose(channel_tail.reshape(layers, taps - 1, model_width), (1, 0, 2))
    mtails = jnp.transpose(matrix_tail.reshape(layers, taps - 1, 2 * state_width), (1, 0, 2))
    hidden = last_hidden.reshape(seq_n, 1, width)

    dims = (
        layers, heads_n, seq_n, members, head_dev, head_width, width, channels, pair, taps
    )
    vmem = pl.BlockSpec(memory_space=pltpu.VMEM)
    smem = pl.BlockSpec(memory_space=pltpu.SMEM)
    anyw = pl.BlockSpec(memory_space=pl.ANY)
    V = pltpu.VMEM
    dma = pltpu.SemaphoreType.DMA
    scratch = [
        V((layers, width, 2, channels), bf16),
        V((layers, channels, width), bf16),
        V((layers, head_dev, width), bf16),
        V((layers, width, 2 * state_width), bf16),
        V((layers, chunks, seq_n, pair, group_heads, head_width, state_width), bf16),
        V((requests, 1, width), f32),
        V((heads_n, tail_rows, channels), f32),
        V((heads_n, tail_rows, 2 * state_width), f32),
        V((seq_n, members, 128), f32),
        V((tail_rows, members, channels), f32),
        V((tail_rows, members, 2 * state_width), f32),
        V((heads_n, chunk_rows, width), f32),
        V((2 * requests, 2 * width), bf16),
        V((2 * requests, channels), f32),
        V((layers, seq_n, 2, members, channels), f32),
        V((layers, seq_n, 2, members, channels), f32),
        V((layers, seq_n, members, 384), f32),
        V((layers, seq_n, members, 384), f32),
        V((128, channels_pad), f32),
        V((channels_pad, 128), f32),
        V((heads_n, tail_rows, channels), f32),
        V((tail_rows, 2 * state_width), f32),
        V((seq_n, 1, width), f32),
        V((members, 128), f32),
        V((layers, members, 3, channels), f32),
        V((layers, seq_n, pair, 3, channels), f32),
        V((layers, seq_n, members, channels), f32),
        V((layers, members, channels), f32),
        V((layers, devices, members, 128), f32),
        V((requests, channels), f32),
        V((layers, heads_n, chunk_rows, width), f32),
        V((layers, heads_n, chunk_rows, width), f32),
        V((layers, heads_n, chunk_rows, width), f32),
        dma((3 * layers + 2 + 2 * steps,)),
        dma((steps, heads_n)),
        dma((steps, heads_n)),
        dma((devices,)),
        dma((devices,)),
        dma((seq_n,)),
        dma((seq_n,)),
        dma((heads_n,)),
        dma((heads_n,)),
        dma((heads_n,)),
        dma((heads_n,)),
        dma((layers, seq_n)),
        dma((layers, seq_n)),
        dma((layers, seq_n)),
        dma((layers, seq_n)),
        dma((layers, seq_n)),
        dma((layers, seq_n)),
        dma((layers, devices)),
        dma((layers, devices)),
        dma((layers, heads_n)),
        dma((layers, heads_n)),
        dma((layers, heads_n)),
        dma((layers, heads_n)),
        dma((steps, seq_n)),
        dma((steps, seq_n)),
        dma((layers, seq_n)),
        dma((layers, seq_n)),
    ] + [V((members, group_heads, head_width, state_width), bf16) for _ in range(steps)]
    decoded, raw, vectors = pl.pallas_call(
        functools.partial(kernel, dims),
        out_shape=(
            jax.ShapeDtypeStruct((share_rows, width), bf16),
            jax.ShapeDtypeStruct(
                (layers, 1, capacity, head_dev, head_width, state_width), bf16
            ),
            jax.ShapeDtypeStruct((layers, capacity, 3, channels), f32),
        ),
        in_specs=[
            smem, anyw, vmem, vmem, vmem, anyw, anyw, anyw,
            vmem, vmem, vmem, vmem, vmem, vmem, anyw,
        ],
        out_specs=(vmem, anyw, anyw),
        scratch_shapes=scratch,
        compiler_params=pltpu.CompilerParams(
            collective_id=0, has_side_effects=True, vmem_limit_bytes=58 * 1024 * 1024
        ),
        cost_estimate=pl.CostEstimate(
            flops=4 * requests * width * channels * 3 * layers,
            bytes_accessed=30_000_000,
            transcendentals=0,
        ),
        name="handover",
    )(
        groups,
        final_state,
        tails,
        mtails,
        hidden,
        input_weight,
        jnp.swapaxes(step_weight, 1, 2),
        matrix_weight,
        channel_conv,
        matrix_conv,
        step_bias,
        decay_log,
        skip_gain,
        norm_gain,
        output_weight,
    )
    block = (1, 1, capacity, group_heads, head_width, state_width)
    new_state, decoded = pl.pallas_call(
        functools.partial(
            update_kernel, (capacity, group_heads * head_width, state_width, channels)
        ),
        grid=(layers, chunks),
        out_shape=(
            jax.ShapeDtypeStruct(raw.shape, bf16),
            jax.ShapeDtypeStruct(decoded.shape, bf16),
        ),
        in_specs=[
            pl.BlockSpec((1, capacity, 3, channels), lambda l, c: (l, 0, 0, 0)),
            pl.BlockSpec(block, lambda l, c: (l, 0, 0, c, 0, 0)),
            pl.BlockSpec((share_rows, width), lambda l, c: (0, 0)),
        ],
        out_specs=(
            pl.BlockSpec(block, lambda l, c: (l, 0, 0, c, 0, 0)),
            pl.BlockSpec((share_rows, width), lambda l, c: (0, 0)),
        ),
        scratch_shapes=[V((128, channels_pad), f32), V((channels_pad, 128), f32)],
        compiler_params=pltpu.CompilerParams(vmem_limit_bytes=32 * 1024 * 1024),
        name="update",
    )(vectors, raw, decoded)
    return decoded, new_state


def solution(mesh):
    return jax.shard_map(
        on_device,
        mesh=mesh,
        in_specs=(
            P(None, ("groups", "seq", "heads"), None, None, None, None),
            P(None, ("groups", "seq", "heads"), None, None, None),
            P(("groups", "seq", "heads"), None, None, None, None),
            P(("groups", "seq", "heads"), None, None),
            P(("groups", "seq"), None),
            P(None, "seq", None, "heads"),
            P(None, "seq", "heads"),
            P(None, "seq", None),
            P(None, None, "heads"),
            P(),
            P(None, "heads"),
            P(None, "heads"),
            P(None, "heads"),
            P(None, "heads"),
            P(None, "heads", "seq"),
        ),
        out_specs=(
            P(("groups", "heads"), "seq"),
            P(None, ("groups", "seq"), None, "heads", None, None),
        ),
        check_vma=False,
    )
```
